512 devices in a mesh: ctx: 32 (over y, x), tp: 16 (over z, core).
Axes of the slice: x: 4, y: 8, z: 8, core: 2. Of those that a mesh axis runs over, the one named last changes fastest.
Arguments:
- queries: bfloat16 [16384, 4096], P('ctx', 'tp'), may hold values from -6 to 6
- keys: bfloat16 [16384, 4096], P('ctx', 'tp'), may hold values from -6 to 6
- values: bfloat16 [16384, 8192], P('ctx', 'tp'), may hold values from -6 to 6
- coef_table: float32 [16, 16], P(None, 'tp'), may hold values from 0.25 to 2
- level_index: int32 [16384, 15], P('ctx'), may hold values from 0 to 15
- out_weight: bfloat16 [8192, 4096], P('tp', 'ctx'), may hold values from -0.0625 to 0.0625
Outputs:
- mixed: bfloat16 [16384, 4096], P(('ctx', 'tp'))
The draws below stay inside these ranges and needn't reach their ends.
All inputs are finite; a program needn't handle non-finite values.
Results may differ from the reference program's by a relative error of at most 0.025.
Values may be sent and summed in bfloat16 or wider, within the bound.
No kernel may reach another device: no remote copies, remote signals or barrier semaphores. Data moves between devices by JAX's collectives and lax.ppermute only.
A program may use at most 64 MiB of HBM per device.

```python
import math
import jax
import jax.numpy as jnp
from jax import lax

D = 4096
H = 16
DK = 256
DV = 512
NCOEF = 16
TOK_DEV = 512
TOKENS = 16384
HEAD_DEV = 1
CTX_LOG = 5
TOK_LOG = 9
LEVELS = 15
N_CTX = 32
N_TP = 16


def set_ends(entries, stream_key, least, top_value):
    dims = entries.shape
    index_at = [jax.random.randint(jax.random.fold_in(stream_key, axis), (), 0, dims[axis]) for axis in range(len(dims))]
    entries = entries.at[tuple(index_at)].set(least)
    longest = dims.index(max(dims))
    index_at[longest] = (index_at[longest] + 1) % dims[longest]
    return entries.at[tuple(index_at)].set(top_value)


def steps_of(key, shape, cuts, least, top_value):
    def one(axis_at, parts):
        steps = jax.random.uniform(jax.random.fold_in(jax.random.fold_in(key, 6), axis_at), (parts,), jnp.float32, least / len(cuts), top_value / len(cuts))
        return jnp.repeat(jnp.exp(steps), shape[axis_at] // parts).reshape((-1,) + (1,) * (len(shape) - axis_at - 1))

    gain = one(*cuts[0])
    for cut in cuts[1:]:
        gain = gain * one(*cut)
    return gain


def centred(own_key, dims, spread, most, split=(), kind=jnp.bfloat16):
    result = spread * jax.random.normal(own_key, dims, jnp.float32)
    if split:
        result = result * steps_of(own_key, dims, split, -0.22, 0.18)
    return jnp.clip(result, -most, most).astype(kind)


def setup_inputs(seed: int = 0) -> dict:
    seeds = jax.random.split(jax.random.key(seed), 7)
    return {
        "queries": centred(seeds[0], (TOKENS, H * DK), 1.0, 6.0, ((0, 32), (1, 16))),
        "keys": centred(seeds[1], (TOKENS, H * DK), 1.0, 6.0, ((0, 32), (1, 16))),
        "values": centred(seeds[2], (TOKENS, H * DV), 1.0, 6.0, ((0, 32), (1, 16))),
        "coef_table": jnp.clip(jnp.exp(math.log(2.0) - 2.0794415 * jax.random.uniform(seeds[3], (NCOEF, H), jnp.float32) ** steps_of(seeds[3], (NCOEF, H), ((1, 16),), -0.2, 0.2)), 0.25, 2.0),
        "level_index": set_ends(jax.random.randint(seeds[4], (TOKENS, LEVELS), 0, NCOEF), jax.random.fold_in(seeds[4], 1), 0, NCOEF - 1).astype(jnp.int32),
        "out_weight": centred(seeds[5], (H * DV, D), (H * DV) ** -0.5, 0.0625, ((0, 16), (1, 32))),
    }


def level_weights(lam_block, bits):
    pos = jnp.arange(lam_block.shape[0], dtype=jnp.int32)
    crossed = jnp.bitwise_xor(pos[:, None], pos[None, :])
    level = jnp.zeros(crossed.shape, jnp.int32)
    for i in range(bits):
        level = level + (crossed >= 2 ** i).astype(jnp.int32)
    weight = jnp.zeros(crossed.shape, jnp.float32)
    for lev in range(bits + 1):
        weight = weight + jnp.where(level == lev, lam_block[:, lev][:, None], 0.0)
    return jnp.where(pos[:, None] >= pos[None, :], weight, 0.0)


def reference(queries, keys, values, coef_table, level_index, out_weight):
    inverse_scale = 1.0 / (DK ** 0.5)
    scales = jnp.exp2(-0.5 * jnp.arange(LEVELS).astype(jnp.float32))
    lam = coef_table[level_index] * scales[None, :, None]
    q_heads = queries.reshape(TOKENS, H, DK).transpose(1, 0, 2)
    k_heads = keys.reshape(TOKENS, H, DK).transpose(1, 0, 2)
    v_heads = values.reshape(TOKENS, H, DV).transpose(1, 0, 2)
    lam_heads = lam.transpose(2, 0, 1)

    def one_head(items):
        q_one, k_one, v_one, lam_one = items
        query_block_list = q_one.reshape(N_CTX, TOK_DEV, DK)
        key_block_list = k_one.reshape(N_CTX, TOK_DEV, DK)
        value_block_list = v_one.reshape(N_CTX, TOK_DEV, DV)
        lam_blocks = lam_one.reshape(N_CTX, TOK_DEV, LEVELS)

        def diagonal_block(blk):
            q_b, k_b, v_b, lam_b = blk
            scores = jnp.dot(q_b, k_b.T, preferred_element_type=jnp.float32) * inverse_scale
            attn = (scores * level_weights(lam_b, TOK_LOG)).astype(jnp.bfloat16)
            return jnp.dot(attn, v_b, preferred_element_type=jnp.float32)

        total = lax.map(diagonal_block, (query_block_list, key_block_list, value_block_list, lam_blocks))
        running_state = jnp.einsum('xbl,xbd->xld', key_block_list.astype(jnp.float32), value_block_list.astype(jnp.float32))
        block_ids = jnp.arange(N_CTX, dtype=jnp.int32)
        for bit in range(CTX_LOG):
            grouped = running_state.reshape(N_CTX // 2 ** (bit + 1), 2, 2 ** bit, DK, DV)
            left = jnp.sum(grouped[:, 0], axis=1)
            sibling_node = jnp.repeat(left, 2 ** (bit + 1), axis=0).astype(jnp.bfloat16)
            outer_product = jnp.einsum('aug,agf->auf', query_block_list.astype(jnp.float32), sibling_node.astype(jnp.float32))
            setbit = ((block_ids >> bit) & 1).astype(jnp.float32)
            factor = lam_blocks[:, :, TOK_LOG + 1 + bit] * inverse_scale * setbit[:, None]
            total = total + outer_product * factor[:, :, None]
        return total.reshape(TOKENS, DV).astype(jnp.bfloat16)

    head_out = lax.map(one_head, (q_heads, k_heads, v_heads, lam_heads))
    attended = head_out.transpose(1, 0, 2).reshape(TOKENS, H * DV)
    width = HEAD_DEV * DV
    summed = jnp.zeros((TOKENS, D), jnp.float32)
    for group in range(N_TP):
        part = jnp.dot(attended[:, group * width:(group + 1) * width], out_weight[group * width:(group + 1) * width], preferred_element_type=jnp.float32).astype(jnp.bfloat16)
        part = lax.optimization_barrier(part)
        summed = summed + part.astype(jnp.float32)
    return summed.astype(jnp.bfloat16)
```

```python
import functools

import jax
import jax.numpy as jnp
from jax import lax
from jax.experimental import pallas as pl
from jax.experimental.pallas import tpu as pltpu
from jax.sharding import Mesh, PartitionSpec as P

F32, BF16 = jnp.float32, jnp.bfloat16
QUAD = ("zl", "core")
TP = ("zh", "zl", "core")
CTX = ("y", "x")
VMEM = pl.BlockSpec(memory_space=pltpu.VMEM)
SMEM = pl.BlockSpec(memory_space=pltpu.SMEM)
PARAMS = pltpu.CompilerParams(vmem_limit_bytes=48 * 1024 * 1024)


def shifted(value, axis, by):
    n = lax.axis_size(axis)
    return lax.ppermute(value, axis, [(i, (i + by) % n) for i in range(n)])


def flipped(value, axis):
    return lax.ppermute(value, axis, [(0, 1), (1, 0)])


def local_kernel(coef_ref, index_ref, q_ref, k_ref, v_ref, local_ref, lam_ref):
    index = index_ref[...]
    lam = jnp.zeros(index.shape, F32)
    for row in range(coef_ref.shape[0]):
        lam = jnp.where(index == row, coef_ref[row, 0], lam)
    level_of = lax.broadcasted_iota(jnp.int32, index.shape, 1).astype(F32)
    lam = lam * jnp.exp2(-0.5 * level_of)
    lam_ref[...] = lam
    inverse_scale = 1.0 / q_ref.shape[1] ** 0.5
    tile = 128
    t = lax.broadcasted_iota(jnp.int32, (tile, tile), 0)
    s = lax.broadcasted_iota(jnp.int32, (tile, tile), 1)
    crossed = jnp.bitwise_xor(t, s)
    causal = t >= s
    for i in range(q_ref.shape[0] // tile):
        rows = slice(i * tile, (i + 1) * tile)
        lam_rows = lam[rows]
        scores = lax.dot_general(
            q_ref[rows, :], k_ref[: (i + 1) * tile, :], (((1,), (1,)), ((), ())), preferred_element_type=F32
        )
        scores = scores * inverse_scale
        pieces = []
        for j in range(i):
            level = 7 + (i ^ j).bit_length()
            pieces.append(scores[:, j * tile : (j + 1) * tile] * lam_rows[:, level : level + 1])
        weight = jnp.broadcast_to(lam_rows[:, 0:1], (tile, tile))
        for bit in range(7):
            weight = jnp.where(crossed >= 2**bit, lam_rows[:, bit + 1 : bit + 2], weight)
        weight = jnp.where(causal, weight, 0.0)
        pieces.append(scores[:, i * tile :] * weight)
        attn = jnp.concatenate([piece.astype(BF16) for piece in pieces], axis=1)
        local_ref[rows, :] = jnp.dot(attn, v_ref[: (i + 1) * tile, :], preferred_element_type=F32)


def inter_kernel(base, bits_ref, local_ref, lam_ref, q_ref, near_ref, pair_ref, far_ref, o_ref):
    q = q_ref[...]
    inverse_scale = 1.0 / q.shape[1] ** 0.5
    total = local_ref[...]
    count = 2 + far_ref.shape[1]
    for bit in range(count):
        if bit == 0:
            node = near_ref[...]
        elif bit == 1:
            node = pair_ref[...]
        else:
            node = jnp.concatenate([far_ref[i, bit - 2] for i in range(far_ref.shape[0])], axis=0)
        setbit = (bits_ref[0] >> bit & 1).astype(F32)
        factor = lam_ref[:, base + bit : base + bit + 1] * inverse_scale * setbit
        total = total + jnp.dot(q, node, preferred_element_type=F32) * factor
    o_ref[...] = total.astype(BF16)


def project_kernel(flip_ref, o0_ref, o1_ref, o2_ref, o3_ref, w_ref, part_ref):
    total = None
    for j, o_ref in enumerate((o0_ref, o1_ref, o2_ref, o3_ref)):
        k = jnp.bitwise_xor(flip_ref[0], j)
        w = jnp.concatenate([w_ref[0, k], w_ref[1, k]], axis=1)
        term = jnp.dot(o_ref[...], w, preferred_element_type=F32)
        total = term if total is None else total + term
    part_ref[...] = total.astype(BF16)


def sum_kernel(got_ref, out_ref):
    quads, members, _, columns = got_ref.shape
    for u in range(members):
        total = got_ref[0, u].astype(F32)
        for i in range(1, quads):
            total = total + got_ref[i, u].astype(F32)
        total = total.astype(BF16)
        for block in range(columns // 128):
            start = (block * members + u) * 128
            out_ref[:, start : start + 128] = total[:, block * 128 : (block + 1) * 128]


def on_device(queries, keys, values, coef_table, level_index, out_weight):
    rows, key_size = queries.shape
    value_size = values.shape[1]
    x, y = lax.axis_index("x"), lax.axis_index("y")
    u = lax.axis_index(QUAD)
    nx, ny, nu = lax.axis_size("x"), lax.axis_size("y"), 4

    got = []
    for k in range(nu):
        pairs = [(i * nu + j, (j ^ k) * nu + i) for i in range(nx) for j in range(nu)]
        got.append(lax.ppermute(out_weight, ("x",) + QUAD, pairs))
    weight = jnp.stack(got)

    state = lax.dot_general(keys, values, (((0,), (0,)), ((), ())), preferred_element_type=F32)
    sent = state.astype(BF16)
    after, across, before = shifted(sent, "x", 1), shifted(sent, "x", 2), shifted(sent, "x", -1)

    gathered = lax.all_gather(weight, "y", axis=0)

    local, lam = pl.pallas_call(
        local_kernel,
        out_shape=(
            jax.ShapeDtypeStruct((rows, value_size), F32),
            jax.ShapeDtypeStruct(level_index.shape, F32),
        ),
        in_specs=[SMEM] + [VMEM] * 4,
        out_specs=(VMEM, VMEM),
        compiler_params=PARAMS,
    )(coef_table, level_index, queries, keys, values)

    piece = key_size // nx
    start = x * piece
    quarter = lax.dynamic_slice_in_dim(state, start, piece)
    for other in (after, across, before):
        quarter = quarter + lax.dynamic_slice_in_dim(other, start, piece).astype(F32)
    pair = (across.astype(F32) + jnp.where(x == 2, after, before).astype(F32)).astype(BF16)
    row_sums = lax.all_gather(quarter.astype(BF16), "y", axis=0).astype(F32)
    far = []
    for bit in range(ny.bit_length() - 1):
        first = ((y >> bit) - 1) << bit
        source = jnp.arange(ny)
        mine = (source >= first) & (source < first + 2**bit)
        far.append(jnp.sum(jnp.where(mine[:, None, None], row_sums, 0.0), axis=0))
    far = lax.all_gather(jnp.stack(far).astype(BF16), "x", axis=0)

    levels = level_index.shape[1]
    block = lax.axis_index(CTX).astype(jnp.int32).reshape(1)
    o = pl.pallas_call(
        functools.partial(inter_kernel, levels - 2 - far.shape[1]),
        out_shape=jax.ShapeDtypeStruct((rows, value_size), BF16),
        in_specs=[SMEM] + [VMEM] * 6,
        out_specs=VMEM,
        compiler_params=PARAMS,
    )(block, local, lam, queries, after, pair, far)

    o_z = flipped(o, "zl")
    o_c = flipped(o, "core")
    o_zc = flipped(o_z, "core")
    flip = jnp.bitwise_xor(x, u).astype(jnp.int32).reshape(1)
    width = out_weight.shape[1]
    whole = pl.BlockSpec((rows, value_size), lambda i: (0, 0))
    part = pl.pallas_call(
        project_kernel,
        grid=(ny // 2,),
        out_shape=jax.ShapeDtypeStruct((rows, ny * width), BF16),
        in_specs=[SMEM]
        + [whole] * 4
        + [pl.BlockSpec((2, nu, value_size, width), lambda i: (i, 0, 0, 0))],
        out_specs=pl.BlockSpec((rows, 2 * width), lambda i: (0, i)),
        compiler_params=PARAMS,
    )(flip, o, o_c, o_z, o_zc, gathered)

    n = lax.axis_size(TP)
    back = lax.all_to_all(part, TP, 0, 0, tiled=True)
    return pl.pallas_call(
        sum_kernel,
        out_shape=jax.ShapeDtypeStruct((rows // n, nu * ny * width), BF16),
        in_specs=[VMEM],
        out_specs=VMEM,
        compiler_params=PARAMS,
    )(back.reshape(n // nu, nu, rows // n, ny * width))


def solution(mesh):
    split = Mesh(mesh.devices.reshape(8, 4, 4, 2, 2), CTX + TP)
    in_specs = (P(CTX, TP), P(CTX, TP), P(CTX, TP), P(None, TP), P(CTX, None), P(TP, CTX))
    out_specs = P(CTX + TP, None)
    return jax.shard_map(on_device, mesh=split, in_specs=in_specs, out_specs=out_specs, check_vma=False)
```

```python
import functools

import jax
import jax.numpy as jnp
from jax import lax
from jax.experimental import pallas as pl
from jax.experimental.pallas import tpu as pltpu
from jax.sharding import Mesh, PartitionSpec as P

F32, BF16 = jnp.float32, jnp.bfloat16
QUAD = ("zl", "core")
TP = ("zh", "zl", "core")
CTX = ("y", "x")
VMEM = pl.BlockSpec(memory_space=pltpu.VMEM)
SMEM = pl.BlockSpec(memory_space=pltpu.SMEM)
PARAMS = pltpu.CompilerParams(vmem_limit_bytes=48 * 1024 * 1024)


def shifted(value, axis, by):
    n = lax.axis_size(axis)
    return lax.ppermute(value, axis, [(i, (i + by) % n) for i in range(n)])


def crossed(value, axis, by):
    return lax.ppermute(value, axis, [(i, i ^ by) for i in range(lax.axis_size(axis))])


def flipped(value, axis):
    return lax.ppermute(value, axis, [(0, 1), (1, 0)])


def local_kernel(coef_ref, index_ref, q_ref, k_ref, v_ref, local_ref, lam_ref):
    index = index_ref[...]
    lam = jnp.zeros(index.shape, F32)
    for row in range(coef_ref.shape[0]):
        lam = jnp.where(index == row, coef_ref[row, 0], lam)
    level_of = lax.broadcasted_iota(jnp.int32, index.shape, 1).astype(F32)
    lam = lam * jnp.exp2(-0.5 * level_of)
    lam_ref[...] = lam
    inverse_scale = 1.0 / q_ref.shape[1] ** 0.5
    tile = 128
    t = lax.broadcasted_iota(jnp.int32, (tile, tile), 0)
    s = lax.broadcasted_iota(jnp.int32, (tile, tile), 1)
    crossed = jnp.bitwise_xor(t, s)
    causal = t >= s
    for i in range(q_ref.shape[0] // tile):
        rows = slice(i * tile, (i + 1) * tile)
        lam_rows = lam[rows]
        scores = lax.dot_general(
            q_ref[rows, :], k_ref[: (i + 1) * tile, :], (((1,), (1,)), ((), ())), preferred_element_type=F32
        )
        scores = scores * inverse_scale
        pieces = []
        for j in range(i):
            level = 7 + (i ^ j).bit_length()
            pieces.append(scores[:, j * tile : (j + 1) * tile] * lam_rows[:, level : level + 1])
        weight = jnp.broadcast_to(lam_rows[:, 0:1], (tile, tile))
        for bit in range(7):
            weight = jnp.where(crossed >= 2**bit, lam_rows[:, bit + 1 : bit + 2], weight)
        weight = jnp.where(causal, weight, 0.0)
        pieces.append(scores[:, i * tile :] * weight)
        attn = jnp.concatenate([piece.astype(BF16) for piece in pieces], axis=1)
        local_ref[rows, :] = jnp.dot(attn, v_ref[: (i + 1) * tile, :], preferred_element_type=F32)


def inter_kernel(base, bits_ref, local_ref, lam_ref, q_ref, near_ref, pair_ref, far_ref, o_ref):
    q = q_ref[...]
    inverse_scale = 1.0 / q.shape[1] ** 0.5
    total = local_ref[...]
    count = 2 + far_ref.shape[1]
    for bit in range(count):
        if bit == 0:
            node = near_ref[...]
        elif bit == 1:
            node = pair_ref[...]
        else:
            node = jnp.concatenate([far_ref[i, bit - 2] for i in range(far_ref.shape[0])], axis=0)
        setbit = (bits_ref[0] >> bit & 1).astype(F32)
        factor = lam_ref[:, base + bit : base + bit + 1] * inverse_scale * setbit
        total = total + jnp.dot(q, node, preferred_element_type=F32) * factor
    o_ref[...] = total.astype(BF16)


def project_kernel(flip_ref, o0_ref, o1_ref, o2_ref, o3_ref, w_ref, part_ref):
    total = None
    for j, o_ref in enumerate((o0_ref, o1_ref, o2_ref, o3_ref)):
        k = jnp.bitwise_xor(flip_ref[0], j)
        w = jnp.concatenate([w_ref[0, k], w_ref[1, k]], axis=1)
        term = jnp.dot(o_ref[...], w, preferred_element_type=F32)
        total = term if total is None else total + term
    part_ref[...] = total.astype(BF16)


def sum_kernel(got_ref, out_ref):
    quads, members, _, columns = got_ref.shape
    for u in range(members):
        total = got_ref[0, u].astype(F32)
        for i in range(1, quads):
            total = total + got_ref[i, u].astype(F32)
        total = total.astype(BF16)
        for block in range(columns // 128):
            start = (block * members + u) * 128
            out_ref[:, start : start + 128] = total[:, block * 128 : (block + 1) * 128]


def on_device(queries, keys, values, coef_table, level_index, out_weight):
    rows, key_size = queries.shape
    value_size = values.shape[1]
    x = lax.axis_index("x")
    u = lax.axis_index(QUAD)
    nx, ny, nu = lax.axis_size("x"), lax.axis_size("y"), 4

    state = lax.dot_general(keys, values, (((0,), (0,)), ((), ())), preferred_element_type=F32)
    sent = state.astype(BF16)
    after, across, before = shifted(sent, "x", 1), shifted(sent, "x", 2), shifted(sent, "x", -1)

    got = []
    for k in range(nu):
        pairs = [(i * nu + j, (j ^ k) * nu + i) for i in range(nx) for j in range(nu)]
        got.append(lax.ppermute(out_weight, ("x",) + QUAD, pairs))
    *got, after, before = lax.optimization_barrier((*got, after, before))
    weight = jnp.stack(got)

    gathered = lax.all_gather(weight, "y", axis=0)

    local, lam = pl.pallas_call(
        local_kernel,
        out_shape=(
            jax.ShapeDtypeStruct((rows, value_size), F32),
            jax.ShapeDtypeStruct(level_index.shape, F32),
        ),
        in_specs=[SMEM] + [VMEM] * 4,
        out_specs=(VMEM, VMEM),
        compiler_params=PARAMS,
    )(coef_table, level_index, queries, keys, values)

    piece = key_size // nx
    start = x * piece
    quarter = lax.dynamic_slice_in_dim(state, start, piece)
    for other in (after, across, before):
        quarter = quarter + lax.dynamic_slice_in_dim(other, start, piece).astype(F32)
    pair = (across.astype(F32) + jnp.where(x == 2, after, before).astype(F32)).astype(BF16)
    beside = crossed(quarter.astype(BF16), "y", 1)
    both = (quarter + beside.astype(F32)).astype(BF16)
    third, fourth, fifth = crossed(both, "y", 2), crossed(both, "y", 4), crossed(both, "y", 6)
    far = [beside, third, (fourth.astype(F32) + fifth.astype(F32)).astype(BF16)]
    far = lax.all_gather(jnp.stack(far), "x", axis=0)

    levels = level_index.shape[1]
    block = lax.axis_index(CTX).astype(jnp.int32).reshape(1)
    o = pl.pallas_call(
        functools.partial(inter_kernel, levels - 2 - far.shape[1]),
        out_shape=jax.ShapeDtypeStruct((rows, value_size), BF16),
        in_specs=[SMEM] + [VMEM] * 6,
        out_specs=VMEM,
        compiler_params=PARAMS,
    )(block, local, lam, queries, after, pair, far)

    o_z = flipped(o, "zl")
    o_c = flipped(o, "core")
    o_zc = flipped(o_z, "core")
    flip = jnp.bitwise_xor(x, u).astype(jnp.int32).reshape(1)
    width = out_weight.shape[1]
    whole = pl.BlockSpec((rows, value_size), lambda i: (0, 0))
    part = pl.pallas_call(
        project_kernel,
        grid=(ny // 2,),
        out_shape=jax.ShapeDtypeStruct((rows, ny * width), BF16),
        in_specs=[SMEM]
        + [whole] * 4
        + [pl.BlockSpec((2, nu, value_size, width), lambda i: (i, 0, 0, 0))],
        out_specs=pl.BlockSpec((rows, 2 * width), lambda i: (0, i)),
        compiler_params=PARAMS,
    )(flip, o, o_c, o_z, o_zc, gathered)

    n = lax.axis_size(TP)
    back = lax.all_to_all(part, TP, 0, 0, tiled=True)
    return pl.pallas_call(
        sum_kernel,
        out_shape=jax.ShapeDtypeStruct((rows // n, nu * ny * width), BF16),
        in_specs=[VMEM],
        out_specs=VMEM,
        compiler_params=PARAMS,
    )(back.reshape(n // nu, nu, rows // n, ny * width))


def solution(mesh):
    split = Mesh(mesh.devices.reshape(8, 4, 4, 2, 2), CTX + TP)
    in_specs = (P(CTX, TP), P(CTX, TP), P(CTX, TP), P(None, TP), P(CTX, None), P(TP, CTX))
    out_specs = P(CTX + TP, None)
    return jax.shard_map(on_device, mesh=split, in_specs=in_specs, out_specs=out_specs, check_vma=False)
```

```python
import functools

import jax
import jax.numpy as jnp
from jax import lax
from jax.experimental import pallas as pl
from jax.experimental.pallas import tpu as pltpu
from jax.sharding import Mesh, PartitionSpec as P

F32, BF16 = jnp.float32, jnp.bfloat16
QUAD = ("zl", "core")
TP = ("zh", "zl", "core")
CTX = ("y", "x")
VMEM = pl.BlockSpec(memory_space=pltpu.VMEM)
SMEM = pl.BlockSpec(memory_space=pltpu.SMEM)
PARAMS = pltpu.CompilerParams(vmem_limit_bytes=48 * 1024 * 1024)


def shifted(value, axis, by):
    n = lax.axis_size(axis)
    return lax.ppermute(value, axis, [(i, (i + by) % n) for i in range(n)])


def crossed(value, axis, by):
    return lax.ppermute(value, axis, [(i, i ^ by) for i in range(lax.axis_size(axis))])


def flipped(value, axis):
    return lax.ppermute(value, axis, [(0, 1), (1, 0)])


def local_kernel(coef_ref, index_ref, q_ref, k_ref, v_ref, local_ref, lam_ref):
    index = index_ref[...]
    lam = jnp.zeros(index.shape, F32)
    for row in range(coef_ref.shape[0]):
        lam = jnp.where(index == row, coef_ref[row, 0], lam)
    level_of = lax.broadcasted_iota(jnp.int32, index.shape, 1).astype(F32)
    lam = lam * jnp.exp2(-0.5 * level_of)
    lam_ref[...] = lam
    inverse_scale = 1.0 / q_ref.shape[1] ** 0.5
    tile = 128
    t = lax.broadcasted_iota(jnp.int32, (tile, tile), 0)
    s = lax.broadcasted_iota(jnp.int32, (tile, tile), 1)
    crossed = jnp.bitwise_xor(t, s)
    causal = t >= s
    for i in range(q_ref.shape[0] // tile):
        rows = slice(i * tile, (i + 1) * tile)
        lam_rows = lam[rows]
        scores = lax.dot_general(
            q_ref[rows, :], k_ref[: (i + 1) * tile, :], (((1,), (1,)), ((), ())), preferred_element_type=F32
        )
        scores = scores * inverse_scale
        pieces = []
        for j in range(i):
            level = 7 + (i ^ j).bit_length()
            pieces.append(scores[:, j * tile : (j + 1) * tile] * lam_rows[:, level : level + 1])
        weight = jnp.broadcast_to(lam_rows[:, 0:1], (tile, tile))
        for bit in range(7):
            weight = jnp.where(crossed >= 2**bit, lam_rows[:, bit + 1 : bit + 2], weight)
        weight = jnp.where(causal, weight, 0.0)
        pieces.append(scores[:, i * tile :] * weight)
        attn = jnp.concatenate([piece.astype(BF16) for piece in pieces], axis=1)
        local_ref[rows, :] = jnp.dot(attn, v_ref[: (i + 1) * tile, :], preferred_element_type=F32)


def inter_kernel(base, bits_ref, local_ref, lam_ref, q_ref, near_ref, pair_ref, far_ref, o_ref):
    q = q_ref[...]
    inverse_scale = 1.0 / q.shape[1] ** 0.5
    total = local_ref[...]
    count = 2 + far_ref.shape[1]
    for bit in range(count):
        if bit == 0:
            node = near_ref[...]
        elif bit == 1:
            node = pair_ref[...]
        else:
            node = jnp.concatenate([far_ref[i, bit - 2] for i in range(far_ref.shape[0])], axis=0)
        setbit = (bits_ref[0] >> bit & 1).astype(F32)
        factor = lam_ref[:, base + bit : base + bit + 1] * inverse_scale * setbit
        total = total + jnp.dot(q, node, preferred_element_type=F32) * factor
    o_ref[...] = total.astype(BF16)


def project_kernel(flip_ref, o0_ref, o1_ref, o2_ref, o3_ref, w_ref, part_ref):
    total = None
    for j, o_ref in enumerate((o0_ref, o1_ref, o2_ref, o3_ref)):
        k = jnp.bitwise_xor(flip_ref[0], j)
        w = jnp.concatenate([w_ref[0, k], w_ref[1, k]], axis=1)
        term = jnp.dot(o_ref[...], w, preferred_element_type=F32)
        total = term if total is None else total + term
    part_ref[...] = total.astype(BF16)


def sum_kernel(got_ref, out_ref):
    quads, members, _, columns = got_ref.shape
    for u in range(members):
        total = got_ref[0, u].astype(F32)
        for i in range(1, quads):
            total = total + got_ref[i, u].astype(F32)
        total = total.astype(BF16)
        for block in range(columns // 128):
            start = (block * members + u) * 128
            out_ref[:, start : start + 128] = total[:, block * 128 : (block + 1) * 128]


def on_device(queries, keys, values, coef_table, level_index, out_weight):
    rows, key_size = queries.shape
    value_size = values.shape[1]
    x = lax.axis_index("x")
    u = lax.axis_index(QUAD)
    nx, ny, nu = lax.axis_size("x"), lax.axis_size("y"), 4

    state = lax.dot_general(keys, values, (((0,), (0,)), ((), ())), preferred_element_type=F32)
    sent = state.astype(BF16)
    piece = key_size // nx
    quarter = lax.dynamic_slice_in_dim(state, x * piece, piece)
    parts = []
    for by in range(1, nx):
        mine = lax.dynamic_slice_in_dim(sent, (x + by) % nx * piece, piece)
        parts.append(shifted(mine, "x", by))

    got = []
    for k in range(nu):
        pairs = [(i * nu + j, (j ^ k) * nu + i) for i in range(nx) for j in range(nu)]
        got.append(lax.ppermute(out_weight, ("x",) + QUAD, pairs))
    for part in parts:
        quarter = quarter + part.astype(F32)
    beside = crossed(quarter.astype(BF16), "y", 1)
    local, lam = pl.pallas_call(
        local_kernel,
        out_shape=(
            jax.ShapeDtypeStruct((rows, value_size), F32),
            jax.ShapeDtypeStruct(level_index.shape, F32),
        ),
        in_specs=[SMEM] + [VMEM] * 4,
        out_specs=(VMEM, VMEM),
        compiler_params=PARAMS,
    )(coef_table, level_index, queries, keys, values)

    *got, beside, local = lax.optimization_barrier((*got, beside, local))
    weight = jnp.stack(got)
    gathered = lax.all_gather(weight, "y", axis=0)

    late, beside = lax.optimization_barrier((sent, beside))
    near = crossed(late, "x", 1)
    pair = crossed((state + near.astype(F32)).astype(BF16), "x", 2)

    both = (quarter + beside.astype(F32)).astype(BF16)
    third, fourth, fifth = crossed(both, "y", 2), crossed(both, "y", 4), crossed(both, "y", 6)
    far = [beside, third, (fourth.astype(F32) + fifth.astype(F32)).astype(BF16)]
    far = lax.all_gather(jnp.stack(far), "x", axis=0)

    levels = level_index.shape[1]
    block = lax.axis_index(CTX).astype(jnp.int32).reshape(1)
    o = pl.pallas_call(
        functools.partial(inter_kernel, levels - 2 - far.shape[1]),
        out_shape=jax.ShapeDtypeStruct((rows, value_size), BF16),
        in_specs=[SMEM] + [VMEM] * 6,
        out_specs=VMEM,
        compiler_params=PARAMS,
    )(block, local, lam, queries, near, pair, far)

    o_z = flipped(o, "zl")
    o_c = flipped(o, "core")
    o_zc = flipped(o_z, "core")
    flip = jnp.bitwise_xor(x, u).astype(jnp.int32).reshape(1)
    width = out_weight.shape[1]
    whole = pl.BlockSpec((rows, value_size), lambda i: (0, 0))
    part = pl.pallas_call(
        project_kernel,
        grid=(ny // 2,),
        out_shape=jax.ShapeDtypeStruct((rows, ny * width), BF16),
        in_specs=[SMEM]
        + [whole] * 4
        + [pl.BlockSpec((2, nu, value_size, width), lambda i: (i, 0, 0, 0))],
        out_specs=pl.BlockSpec((rows, 2 * width), lambda i: (0, i)),
        compiler_params=PARAMS,
    )(flip, o, o_c, o_z, o_zc, gathered)

    n = lax.axis_size(TP)
    back = lax.all_to_all(part, TP, 0, 0, tiled=True)
    return pl.pallas_call(
        sum_kernel,
        out_shape=jax.ShapeDtypeStruct((rows // n, nu * ny * width), BF16),
        in_specs=[VMEM],
        out_specs=VMEM,
        compiler_params=PARAMS,
    )(back.reshape(n // nu, nu, rows // n, ny * width))


def solution(mesh):
    split = Mesh(mesh.devices.reshape(8, 4, 4, 2, 2), CTX + TP)
    in_specs = (P(CTX, TP), P(CTX, TP), P(CTX, TP), P(None, TP), P(CTX, None), P(TP, CTX))
    out_specs = P(CTX + TP, None)
    return jax.shard_map(on_device, mesh=split, in_specs=in_specs, out_specs=out_specs, check_vma=False)
```

```python
import functools

import jax
import jax.numpy as jnp
from jax import lax
from jax.experimental import pallas as pl
from jax.experimental.pallas import tpu as pltpu
from jax.sharding import Mesh, PartitionSpec as P

F32, BF16 = jnp.float32, jnp.bfloat16
QUAD = ("zl", "core")
TP = ("zh", "zl", "core")
CTX = ("y", "x")
VMEM = pl.BlockSpec(memory_space=pltpu.VMEM)
SMEM = pl.BlockSpec(memory_space=pltpu.SMEM)
PARAMS = pltpu.CompilerParams(vmem_limit_bytes=48 * 1024 * 1024)


def shifted(value, axis, by):
    n = lax.axis_size(axis)
    return lax.ppermute(value, axis, [(i, (i + by) % n) for i in range(n)])


def crossed(value, axis, by):
    return lax.ppermute(value, axis, [(i, i ^ by) for i in range(lax.axis_size(axis))])


def flipped(value, axis):
    return lax.ppermute(value, axis, [(0, 1), (1, 0)])


def local_kernel(coef_ref, index_ref, q_ref, k_ref, v_ref, local_ref, lam_ref):
    index = index_ref[...]
    lam = jnp.zeros(index.shape, F32)
    for row in range(coef_ref.shape[0]):
        lam = jnp.where(index == row, coef_ref[row, 0], lam)
    level_of = lax.broadcasted_iota(jnp.int32, index.shape, 1).astype(F32)
    lam = lam * jnp.exp2(-0.5 * level_of)
    lam_ref[...] = lam
    inverse_scale = 1.0 / q_ref.shape[1] ** 0.5
    tile = 128
    t = lax.broadcasted_iota(jnp.int32, (tile, tile), 0)
    s = lax.broadcasted_iota(jnp.int32, (tile, tile), 1)
    crossed = jnp.bitwise_xor(t, s)
    causal = t >= s
    for i in range(q_ref.shape[0] // tile):
        rows = slice(i * tile, (i + 1) * tile)
        lam_rows = lam[rows]
        scores = lax.dot_general(
            q_ref[rows, :], k_ref[: (i + 1) * tile, :], (((1,), (1,)), ((), ())), preferred_element_type=F32
        )
        scores = scores * inverse_scale
        pieces = []
        for j in range(i):
            level = 7 + (i ^ j).bit_length()
            pieces.append(scores[:, j * tile : (j + 1) * tile] * lam_rows[:, level : level + 1])
        weight = jnp.broadcast_to(lam_rows[:, 0:1], (tile, tile))
        for bit in range(7):
            weight = jnp.where(crossed >= 2**bit, lam_rows[:, bit + 1 : bit + 2], weight)
        weight = jnp.where(causal, weight, 0.0)
        pieces.append(scores[:, i * tile :] * weight)
        attn = jnp.concatenate([piece.astype(BF16) for piece in pieces], axis=1)
        local_ref[rows, :] = jnp.dot(attn, v_ref[: (i + 1) * tile, :], preferred_element_type=F32)


def inter_kernel(base, bits_ref, local_ref, lam_ref, q_ref, near_ref, pair_ref, far_ref, o_ref):
    q = q_ref[...]
    inverse_scale = 1.0 / q.shape[1] ** 0.5
    total = local_ref[...]
    count = 2 + far_ref.shape[1]
    for bit in range(count):
        if bit == 0:
            node = near_ref[...]
        elif bit == 1:
            node = pair_ref[...]
        else:
            node = jnp.concatenate([far_ref[i, bit - 2] for i in range(far_ref.shape[0])], axis=0)
        setbit = (bits_ref[0] >> bit & 1).astype(F32)
        factor = lam_ref[:, base + bit : base + bit + 1] * inverse_scale * setbit
        total = total + jnp.dot(q, node, preferred_element_type=F32) * factor
    o_ref[...] = total.astype(BF16)


def project_kernel(flip_ref, o0_ref, o1_ref, o2_ref, o3_ref, w_ref, part_ref):
    total = None
    for j, o_ref in enumerate((o0_ref, o1_ref, o2_ref, o3_ref)):
        k = jnp.bitwise_xor(flip_ref[0], j)
        w = jnp.concatenate([w_ref[0, k], w_ref[1, k]], axis=1)
        term = jnp.dot(o_ref[...], w, preferred_element_type=F32)
        total = term if total is None else total + term
    part_ref[...] = total.astype(BF16)


def sum_kernel(got_ref, out_ref):
    quads, members, _, columns = got_ref.shape
    for u in range(members):
        total = got_ref[0, u].astype(F32)
        for i in range(1, quads):
            total = total + got_ref[i, u].astype(F32)
        total = total.astype(BF16)
        for block in range(columns // 128):
            start = (block * members + u) * 128
            out_ref[:, start : start + 128] = total[:, block * 128 : (block + 1) * 128]


def on_device(queries, keys, values, coef_table, level_index, out_weight):
    rows, key_size = queries.shape
    value_size = values.shape[1]
    x = lax.axis_index("x")
    u = lax.axis_index(QUAD)
    nx, ny, nu = lax.axis_size("x"), lax.axis_size("y"), 4

    state = lax.dot_general(keys, values, (((0,), (0,)), ((), ())), preferred_element_type=F32)
    near = crossed(state.astype(BF16), "x", 1)

    got = []
    for k in range(nu):
        pairs = [(i * nu + j, (j ^ k) * nu + i) for i in range(nx) for j in range(nu)]
        got.append(lax.ppermute(out_weight, ("x",) + QUAD, pairs))
    two = state + near.astype(F32)
    pair = crossed(two.astype(BF16), "x", 2)

    *got, near = lax.optimization_barrier((*got, near))
    weight = jnp.stack(got)
    gathered = lax.all_gather(weight, "y", axis=0)

    local, lam = pl.pallas_call(
        local_kernel,
        out_shape=(
            jax.ShapeDtypeStruct((rows, value_size), F32),
            jax.ShapeDtypeStruct(level_index.shape, F32),
        ),
        in_specs=[SMEM] + [VMEM] * 4,
        out_specs=(VMEM, VMEM),
        compiler_params=PARAMS,
    )(coef_table, level_index, queries, keys, values)

    pair, local = lax.optimization_barrier((pair, local))
    piece = key_size // nx
    four = two + pair.astype(F32)
    quarter = lax.dynamic_slice_in_dim(four, x * piece, piece)
    beside = crossed(quarter.astype(BF16), "y", 1)
    both = (quarter + beside.astype(F32)).astype(BF16)
    third, fourth, fifth = crossed(both, "y", 2), crossed(both, "y", 4), crossed(both, "y", 6)
    far = [beside, third, (fourth.astype(F32) + fifth.astype(F32)).astype(BF16)]
    far = lax.all_gather(jnp.stack(far), "x", axis=0)

    levels = level_index.shape[1]
    block = lax.axis_index(CTX).astype(jnp.int32).reshape(1)
    o = pl.pallas_call(
        functools.partial(inter_kernel, levels - 2 - far.shape[1]),
        out_shape=jax.ShapeDtypeStruct((rows, value_size), BF16),
        in_specs=[SMEM] + [VMEM] * 6,
        out_specs=VMEM,
        compiler_params=PARAMS,
    )(block, local, lam, queries, near, pair, far)

    o_z = flipped(o, "zl")
    o_c = flipped(o, "core")
    o_zc = flipped(o_z, "core")
    flip = jnp.bitwise_xor(x, u).astype(jnp.int32).reshape(1)
    width = out_weight.shape[1]
    whole = pl.BlockSpec((rows, value_size), lambda i: (0, 0))
    part = pl.pallas_call(
        project_kernel,
        grid=(ny // 2,),
        out_shape=jax.ShapeDtypeStruct((rows, ny * width), BF16),
        in_specs=[SMEM]
        + [whole] * 4
        + [pl.BlockSpec((2, nu, value_size, width), lambda i: (i, 0, 0, 0))],
        out_specs=pl.BlockSpec((rows, 2 * width), lambda i: (0, i)),
        compiler_params=PARAMS,
    )(flip, o, o_c, o_z, o_zc, gathered)

    n = lax.axis_size(TP)
    back = lax.all_to_all(part, TP, 0, 0, tiled=True)
    return pl.pallas_call(
        sum_kernel,
        out_shape=jax.ShapeDtypeStruct((rows // n, nu * ny * width), BF16),
        in_specs=[VMEM],
        out_specs=VMEM,
        compiler_params=PARAMS,
    )(back.reshape(n // nu, nu, rows // n, ny * width))


def solution(mesh):
    split = Mesh(mesh.devices.reshape(8, 4, 4, 2, 2), CTX + TP)
    in_specs = (P(CTX, TP), P(CTX, TP), P(CTX, TP), P(None, TP), P(CTX, None), P(TP, CTX))
    out_specs = P(CTX + TP, None)
    return jax.shard_map(on_device, mesh=split, in_specs=in_specs, out_specs=out_specs, check_vma=False)
```

```python
import functools

import jax
import jax.numpy as jnp
from jax import lax
from jax.experimental import pallas as pl
from jax.experimental.pallas import tpu as pltpu
from jax.sharding import Mesh, PartitionSpec as P

F32, BF16 = jnp.float32, jnp.bfloat16
QUAD = ("zl", "core")
TP = ("zh", "zl", "core")
CTX = ("y", "x")
VMEM = pl.BlockSpec(memory_space=pltpu.VMEM)
SMEM = pl.BlockSpec(memory_space=pltpu.SMEM)
PARAMS = pltpu.CompilerParams(vmem_limit_bytes=48 * 1024 * 1024)


def shifted(value, axis, by):
    n = lax.axis_size(axis)
    return lax.ppermute(value, axis, [(i, (i + by) % n) for i in range(n)])


def crossed(value, axis, by):
    return lax.ppermute(value, axis, [(i, i ^ by) for i in range(lax.axis_size(axis))])


def flipped(value, axis):
    return lax.ppermute(value, axis, [(0, 1), (1, 0)])


def local_kernel(coef_ref, index_ref, q_ref, k_ref, v_ref, local_ref, lam_ref):
    index = index_ref[...]
    lam = jnp.zeros(index.shape, F32)
    for row in range(coef_ref.shape[0]):
        lam = jnp.where(index == row, coef_ref[row, 0], lam)
    level_of = lax.broadcasted_iota(jnp.int32, index.shape, 1).astype(F32)
    lam = lam * jnp.exp2(-0.5 * level_of)
    lam_ref[...] = lam
    inverse_scale = 1.0 / q_ref.shape[1] ** 0.5
    tile = 128
    t = lax.broadcasted_iota(jnp.int32, (tile, tile), 0)
    s = lax.broadcasted_iota(jnp.int32, (tile, tile), 1)
    crossed = jnp.bitwise_xor(t, s)
    causal = t >= s
    for i in range(q_ref.shape[0] // tile):
        rows = slice(i * tile, (i + 1) * tile)
        lam_rows = lam[rows]
        scores = lax.dot_general(
            q_ref[rows, :], k_ref[: (i + 1) * tile, :], (((1,), (1,)), ((), ())), preferred_element_type=F32
        )
        scores = scores * inverse_scale
        pieces = []
        for j in range(i):
            level = 7 + (i ^ j).bit_length()
            pieces.append(scores[:, j * tile : (j + 1) * tile] * lam_rows[:, level : level + 1])
        weight = jnp.broadcast_to(lam_rows[:, 0:1], (tile, tile))
        for bit in range(7):
            weight = jnp.where(crossed >= 2**bit, lam_rows[:, bit + 1 : bit + 2], weight)
        weight = jnp.where(causal, weight, 0.0)
        pieces.append(scores[:, i * tile :] * weight)
        attn = jnp.concatenate([piece.astype(BF16) for piece in pieces], axis=1)
        local_ref[rows, :] = jnp.dot(attn, v_ref[: (i + 1) * tile, :], preferred_element_type=F32)


def inter_kernel(base, bits_ref, local_ref, lam_ref, q_ref, near_ref, pair_ref, far_ref, o_ref):
    q = q_ref[...]
    inverse_scale = 1.0 / q.shape[1] ** 0.5
    total = local_ref[...]
    count = 2 + far_ref.shape[1]
    for bit in range(count):
        if bit == 0:
            node = near_ref[...]
        elif bit == 1:
            node = pair_ref[...]
        else:
            node = jnp.concatenate([far_ref[i, bit - 2] for i in range(far_ref.shape[0])], axis=0)
        setbit = (bits_ref[0] >> bit & 1).astype(F32)
        factor = lam_ref[:, base + bit : base + bit + 1] * inverse_scale * setbit
        total = total + jnp.dot(q, node, preferred_element_type=F32) * factor
    o_ref[...] = total.astype(BF16)


def project_kernel(flip_ref, o0_ref, o1_ref, o2_ref, o3_ref, w_ref, part_ref):
    total = None
    for j, o_ref in enumerate((o0_ref, o1_ref, o2_ref, o3_ref)):
        k = jnp.bitwise_xor(flip_ref[0], j)
        w = jnp.concatenate([w_ref[0, k], w_ref[1, k]], axis=1)
        term = jnp.dot(o_ref[...], w, preferred_element_type=F32)
        total = term if total is None else total + term
    part_ref[...] = total.astype(BF16)


def sum_kernel(got_ref, out_ref):
    quads, members, _, columns = got_ref.shape
    for u in range(members):
        total = got_ref[0, u].astype(F32)
        for i in range(1, quads):
            total = total + got_ref[i, u].astype(F32)
        total = total.astype(BF16)
        for block in range(columns // 128):
            start = (block * members + u) * 128
            out_ref[:, start : start + 128] = total[:, block * 128 : (block + 1) * 128]


def on_device(queries, keys, values, coef_table, level_index, out_weight):
    rows, key_size = queries.shape
    value_size = values.shape[1]
    x = lax.axis_index("x")
    u = lax.axis_index(QUAD)
    nx, ny, nu = lax.axis_size("x"), lax.axis_size("y"), 4

    state = lax.dot_general(keys, values, (((0,), (0,)), ((), ())), preferred_element_type=F32)
    near = crossed(state.astype(BF16), "x", 1)

    got = []
    for k in range(nu):
        pairs = [(i * nu + j, (j ^ k) * nu + i) for i in range(nx) for j in range(nu)]
        got.append(lax.ppermute(out_weight, ("x",) + QUAD, pairs))
    near, got[0], got[1] = lax.optimization_barrier((near, got[0], got[1]))
    two = state + near.astype(F32)
    pair = crossed(two.astype(BF16), "x", 2)

    *got, pair = lax.optimization_barrier((*got, pair))
    weight = jnp.stack(got)
    gathered = lax.all_gather(weight, "y", axis=0)

    local, lam = pl.pallas_call(
        local_kernel,
        out_shape=(
            jax.ShapeDtypeStruct((rows, value_size), F32),
            jax.ShapeDtypeStruct(level_index.shape, F32),
        ),
        in_specs=[SMEM] + [VMEM] * 4,
        out_specs=(VMEM, VMEM),
        compiler_params=PARAMS,
    )(coef_table, level_index, queries, keys, values)

    piece = key_size // nx
    four = two + pair.astype(F32)
    quarter = lax.dynamic_slice_in_dim(four, x * piece, piece)
    beside = crossed(quarter.astype(BF16), "y", 1)
    beside, local = lax.optimization_barrier((beside, local))
    both = (quarter + beside.astype(F32)).astype(BF16)
    third, fourth, fifth = crossed(both, "y", 2), crossed(both, "y", 4), crossed(both, "y", 6)
    far = [beside, third, (fourth.astype(F32) + fifth.astype(F32)).astype(BF16)]
    far = lax.all_gather(jnp.stack(far), "x", axis=0)

    levels = level_index.shape[1]
    block = lax.axis_index(CTX).astype(jnp.int32).reshape(1)
    o = pl.pallas_call(
        functools.partial(inter_kernel, levels - 2 - far.shape[1]),
        out_shape=jax.ShapeDtypeStruct((rows, value_size), BF16),
        in_specs=[SMEM] + [VMEM] * 6,
        out_specs=VMEM,
        compiler_params=PARAMS,
    )(block, local, lam, queries, near, pair, far)

    o_z = flipped(o, "zl")
    o_c = flipped(o, "core")
    o_zc = flipped(o_z, "core")
    flip = jnp.bitwise_xor(x, u).astype(jnp.int32).reshape(1)
    width = out_weight.shape[1]
    whole = pl.BlockSpec((rows, value_size), lambda i: (0, 0))
    part = pl.pallas_call(
        project_kernel,
        grid=(ny // 2,),
        out_shape=jax.ShapeDtypeStruct((rows, ny * width), BF16),
        in_specs=[SMEM]
        + [whole] * 4
        + [pl.BlockSpec((2, nu, value_size, width), lambda i: (i, 0, 0, 0))],
        out_specs=pl.BlockSpec((rows, 2 * width), lambda i: (0, i)),
        compiler_params=PARAMS,
    )(flip, o, o_c, o_z, o_zc, gathered)

    n = lax.axis_size(TP)
    back = lax.all_to_all(part, TP, 0, 0, tiled=True)
    return pl.pallas_call(
        sum_kernel,
        out_shape=jax.ShapeDtypeStruct((rows // n, nu * ny * width), BF16),
        in_specs=[VMEM],
        out_specs=VMEM,
        compiler_params=PARAMS,
    )(back.reshape(n // nu, nu, rows // n, ny * width))


def solution(mesh):
    split = Mesh(mesh.devices.reshape(8, 4, 4, 2, 2), CTX + TP)
    in_specs = (P(CTX, TP), P(CTX, TP), P(CTX, TP), P(None, TP), P(CTX, None), P(TP, CTX))
    out_specs = P(CTX + TP, None)
    return jax.shard_map(on_device, mesh=split, in_specs=in_specs, out_specs=out_specs, check_vma=False)
```

```python
import functools

import jax
import jax.numpy as jnp
from jax import lax
from jax.experimental import pallas as pl
from jax.experimental.pallas import tpu as pltpu
from jax.sharding import Mesh, PartitionSpec as P

F32, BF16 = jnp.float32, jnp.bfloat16
QUAD = ("zl", "core")
TP = ("zh", "zl", "core")
CTX = ("y", "x")
VMEM = pl.BlockSpec(memory_space=pltpu.VMEM)
SMEM = pl.BlockSpec(memory_space=pltpu.SMEM)
PARAMS = pltpu.CompilerParams(vmem_limit_bytes=48 * 1024 * 1024)


def shifted(value, axis, by):
    n = lax.axis_size(axis)
    return lax.ppermute(value, axis, [(i, (i + by) % n) for i in range(n)])


def crossed(value, axis, by):
    return lax.ppermute(value, axis, [(i, i ^ by) for i in range(lax.axis_size(axis))])


def flipped(value, axis):
    return lax.ppermute(value, axis, [(0, 1), (1, 0)])


def local_kernel(coef_ref, index_ref, q_ref, k_ref, v_ref, local_ref, lam_ref):
    index = index_ref[...]
    lam = jnp.zeros(index.shape, F32)
    for row in range(coef_ref.shape[0]):
        lam = jnp.where(index == row, coef_ref[row, 0], lam)
    level_of = lax.broadcasted_iota(jnp.int32, index.shape, 1).astype(F32)
    lam = lam * jnp.exp2(-0.5 * level_of)
    lam_ref[...] = lam
    inverse_scale = 1.0 / q_ref.shape[1] ** 0.5
    tile = 128
    t = lax.broadcasted_iota(jnp.int32, (tile, tile), 0)
    s = lax.broadcasted_iota(jnp.int32, (tile, tile), 1)
    crossed = jnp.bitwise_xor(t, s)
    causal = t >= s
    for i in range(q_ref.shape[0] // tile):
        rows = slice(i * tile, (i + 1) * tile)
        lam_rows = lam[rows]
        scores = lax.dot_general(
            q_ref[rows, :], k_ref[: (i + 1) * tile, :], (((1,), (1,)), ((), ())), preferred_element_type=F32
        )
        scores = scores * inverse_scale
        pieces = []
        for j in range(i):
            level = 7 + (i ^ j).bit_length()
            pieces.append(scores[:, j * tile : (j + 1) * tile] * lam_rows[:, level : level + 1])
        weight = jnp.broadcast_to(lam_rows[:, 0:1], (tile, tile))
        for bit in range(7):
            weight = jnp.where(crossed >= 2**bit, lam_rows[:, bit + 1 : bit + 2], weight)
        weight = jnp.where(causal, weight, 0.0)
        pieces.append(scores[:, i * tile :] * weight)
        attn = jnp.concatenate([piece.astype(BF16) for piece in pieces], axis=1)
        local_ref[rows, :] = jnp.dot(attn, v_ref[: (i + 1) * tile, :], preferred_element_type=F32)


def inter_kernel(base, bits_ref, local_ref, lam_ref, q_ref, near_ref, pair_ref, far_ref, o_ref):
    q = q_ref[...]
    inverse_scale = 1.0 / q.shape[1] ** 0.5
    total = local_ref[...]
    count = 2 + far_ref.shape[1]
    for bit in range(count):
        if bit == 0:
            node = near_ref[...]
        elif bit == 1:
            node = pair_ref[...]
        else:
            node = jnp.concatenate([far_ref[i, bit - 2] for i in (0, 2, 1, 3)], axis=0)
        setbit = (bits_ref[0] >> bit & 1).astype(F32)
        factor = lam_ref[:, base + bit : base + bit + 1] * inverse_scale * setbit
        total = total + jnp.dot(q, node, preferred_element_type=F32) * factor
    o_ref[...] = total.astype(BF16)


def project_kernel(flip_ref, o0_ref, o1_ref, o2_ref, o3_ref, w_ref, part_ref):
    total = None
    for j, o_ref in enumerate((o0_ref, o1_ref, o2_ref, o3_ref)):
        k = jnp.bitwise_xor(flip_ref[0], j)
        w = jnp.concatenate([w_ref[0, k], w_ref[1, k]], axis=1)
        term = jnp.dot(o_ref[...], w, preferred_element_type=F32)
        total = term if total is None else total + term
    part_ref[...] = total.astype(BF16)


def sum_kernel(got_ref, out_ref):
    quads, members, _, columns = got_ref.shape
    for u in range(members):
        total = got_ref[0, u].astype(F32)
        for i in range(1, quads):
            total = total + got_ref[i, u].astype(F32)
        total = total.astype(BF16)
        for block in range(columns // 128):
            start = (block * members + u) * 128
            out_ref[:, start : start + 128] = total[:, block * 128 : (block + 1) * 128]


def on_device(queries, keys, values, coef_table, level_index, out_weight):
    rows, key_size = queries.shape
    value_size = values.shape[1]
    x = lax.axis_index("x")
    u = lax.axis_index(QUAD)
    nx, ny, nu = lax.axis_size("x"), lax.axis_size("y"), 4

    state = lax.dot_general(keys, values, (((0,), (0,)), ((), ())), preferred_element_type=F32)
    half, piece = key_size // 2, key_size // nx
    odd, high = x % 2, x // 2
    given = lax.dynamic_slice_in_dim(state, (1 - odd) * half, half).astype(BF16)
    kept = lax.dynamic_slice_in_dim(state, odd * half, half)
    one = crossed(given, "x", 1)

    got = []
    for k in range(nu):
        pairs = [(i * nu + j, (j ^ k) * nu + i) for i in range(nx) for j in range(nu)]
        got.append(lax.ppermute(out_weight, ("x",) + QUAD, pairs))

    *got, one = lax.optimization_barrier((*got, one))
    weight = jnp.stack(got)
    gathered = lax.all_gather(weight, "y", axis=0)

    halves = kept + one.astype(F32)
    given = lax.dynamic_slice_in_dim(halves, (1 - high) * piece, piece).astype(BF16)
    quarter = lax.dynamic_slice_in_dim(halves, high * piece, piece)
    part = crossed(given, "x", 2)
    quarter = quarter + part.astype(F32)
    beside = crossed(quarter.astype(BF16), "y", 1)

    late, part = lax.optimization_barrier((kept.astype(BF16), part))
    rest = crossed(late, "x", 1)
    near = jnp.where(odd == 1, jnp.concatenate([rest, one]), jnp.concatenate([one, rest]))
    pair = crossed((state + near.astype(F32)).astype(BF16), "x", 2)

    local, lam = pl.pallas_call(
        local_kernel,
        out_shape=(
            jax.ShapeDtypeStruct((rows, value_size), F32),
            jax.ShapeDtypeStruct(level_index.shape, F32),
        ),
        in_specs=[SMEM] + [VMEM] * 4,
        out_specs=(VMEM, VMEM),
        compiler_params=PARAMS,
    )(coef_table, level_index, queries, keys, values)

    beside, local = lax.optimization_barrier((beside, local))
    both = (quarter + beside.astype(F32)).astype(BF16)
    third, fourth, fifth = crossed(both, "y", 2), crossed(both, "y", 4), crossed(both, "y", 6)
    far = [beside, third, (fourth.astype(F32) + fifth.astype(F32)).astype(BF16)]
    far = lax.all_gather(jnp.stack(far), "x", axis=0)

    levels = level_index.shape[1]
    block = lax.axis_index(CTX).astype(jnp.int32).reshape(1)
    o = pl.pallas_call(
        functools.partial(inter_kernel, levels - 2 - far.shape[1]),
        out_shape=jax.ShapeDtypeStruct((rows, value_size), BF16),
        in_specs=[SMEM] + [VMEM] * 6,
        out_specs=VMEM,
        compiler_params=PARAMS,
    )(block, local, lam, queries, near, pair, far)

    o_z = flipped(o, "zl")
    o_c = flipped(o, "core")
    o_zc = flipped(o_z, "core")
    flip = jnp.bitwise_xor(x, u).astype(jnp.int32).reshape(1)
    width = out_weight.shape[1]
    whole = pl.BlockSpec((rows, value_size), lambda i: (0, 0))
    part = pl.pallas_call(
        project_kernel,
        grid=(ny // 2,),
        out_shape=jax.ShapeDtypeStruct((rows, ny * width), BF16),
        in_specs=[SMEM]
        + [whole] * 4
        + [pl.BlockSpec((2, nu, value_size, width), lambda i: (i, 0, 0, 0))],
        out_specs=pl.BlockSpec((rows, 2 * width), lambda i: (0, i)),
        compiler_params=PARAMS,
    )(flip, o, o_c, o_z, o_zc, gathered)

    n = lax.axis_size(TP)
    back = lax.all_to_all(part, TP, 0, 0, tiled=True)
    return pl.pallas_call(
        sum_kernel,
        out_shape=jax.ShapeDtypeStruct((rows // n, nu * ny * width), BF16),
        in_specs=[VMEM],
        out_specs=VMEM,
        compiler_params=PARAMS,
    )(back.reshape(n // nu, nu, rows // n, ny * width))


def solution(mesh):
    split = Mesh(mesh.devices.reshape(8, 4, 4, 2, 2), CTX + TP)
    in_specs = (P(CTX, TP), P(CTX, TP), P(CTX, TP), P(None, TP), P(CTX, None), P(TP, CTX))
    out_specs = P(CTX + TP, None)
    return jax.shard_map(on_device, mesh=split, in_specs=in_specs, out_specs=out_specs, check_vma=False)
```

```python
import functools

import jax
import jax.numpy as jnp
from jax import lax
from jax.experimental import pallas as pl
from jax.experimental.pallas import tpu as pltpu
from jax.sharding import Mesh, PartitionSpec as P

F32, BF16 = jnp.float32, jnp.bfloat16
QUAD = ("zl", "core")
TP = ("zh", "zl", "core")
CTX = ("y", "x")
VMEM = pl.BlockSpec(memory_space=pltpu.VMEM)
SMEM = pl.BlockSpec(memory_space=pltpu.SMEM)
PARAMS = pltpu.CompilerParams(vmem_limit_bytes=48 * 1024 * 1024)


def shifted(value, axis, by):
    n = lax.axis_size(axis)
    return lax.ppermute(value, axis, [(i, (i + by) % n) for i in range(n)])


def crossed(value, axis, by):
    return lax.ppermute(value, axis, [(i, i ^ by) for i in range(lax.axis_size(axis))])


def flipped(value, axis):
    return lax.ppermute(value, axis, [(0, 1), (1, 0)])


def local_kernel(coef_ref, index_ref, q_ref, k_ref, v_ref, local_ref, lam_ref):
    index = index_ref[...]
    lam = jnp.zeros(index.shape, F32)
    for row in range(coef_ref.shape[0]):
        lam = jnp.where(index == row, coef_ref[row, 0], lam)
    level_of = lax.broadcasted_iota(jnp.int32, index.shape, 1).astype(F32)
    lam = lam * jnp.exp2(-0.5 * level_of)
    lam_ref[...] = lam
    inverse_scale = 1.0 / q_ref.shape[1] ** 0.5
    tile = 128
    t = lax.broadcasted_iota(jnp.int32, (tile, tile), 0)
    s = lax.broadcasted_iota(jnp.int32, (tile, tile), 1)
    crossed = jnp.bitwise_xor(t, s)
    causal = t >= s
    for i in range(q_ref.shape[0] // tile):
        rows = slice(i * tile, (i + 1) * tile)
        lam_rows = lam[rows]
        scores = lax.dot_general(
            q_ref[rows, :], k_ref[: (i + 1) * tile, :], (((1,), (1,)), ((), ())), preferred_element_type=F32
        )
        scores = scores * inverse_scale
        pieces = []
        for j in range(i):
            level = 7 + (i ^ j).bit_length()
            pieces.append(scores[:, j * tile : (j + 1) * tile] * lam_rows[:, level : level + 1])
        weight = jnp.broadcast_to(lam_rows[:, 0:1], (tile, tile))
        for bit in range(7):
            weight = jnp.where(crossed >= 2**bit, lam_rows[:, bit + 1 : bit + 2], weight)
        weight = jnp.where(causal, weight, 0.0)
        pieces.append(scores[:, i * tile :] * weight)
        attn = jnp.concatenate([piece.astype(BF16) for piece in pieces], axis=1)
        local_ref[rows, :] = jnp.dot(attn, v_ref[: (i + 1) * tile, :], preferred_element_type=F32)


def inter_kernel(base, bits_ref, local_ref, lam_ref, q_ref, near_ref, pair_ref, far_ref, o_ref):
    q = q_ref[...]
    inverse_scale = 1.0 / q.shape[1] ** 0.5
    total = local_ref[...]
    count = 2 + far_ref.shape[1]
    for bit in range(count):
        if bit == 0:
            node = near_ref[...]
        elif bit == 1:
            node = pair_ref[...]
        else:
            node = jnp.concatenate([far_ref[i, bit - 2] for i in (0, 2, 1, 3)], axis=0)
        setbit = (bits_ref[0] >> bit & 1).astype(F32)
        factor = lam_ref[:, base + bit : base + bit + 1] * inverse_scale * setbit
        total = total + jnp.dot(q, node, preferred_element_type=F32) * factor
    o_ref[...] = total.astype(BF16)


def project_kernel(flip_ref, o0_ref, o1_ref, o2_ref, o3_ref, w_ref, part_ref, held_ref, sems):
    copies = []
    for i in range(w_ref.shape[0] // 2):
        blocks = pl.ds(2 * i, 2)
        copies.append(pltpu.make_async_copy(w_ref.at[blocks], held_ref.at[blocks], sems.at[i]))
        copies[-1].start()
    width = 2 * w_ref.shape[3]
    for i, copy in enumerate(copies):
        copy.wait()
        total = None
        for j, o_ref in enumerate((o0_ref, o1_ref, o2_ref, o3_ref)):
            k = jnp.bitwise_xor(flip_ref[0], j)
            w = jnp.concatenate([held_ref[2 * i, k], held_ref[2 * i + 1, k]], axis=1)
            term = jnp.dot(o_ref[...], w, preferred_element_type=F32)
            total = term if total is None else total + term
        part_ref[:, i * width : (i + 1) * width] = total.astype(BF16)


def sum_kernel(got_ref, out_ref):
    quads, members, _, columns = got_ref.shape
    for u in range(members):
        total = got_ref[0, u].astype(F32)
        for i in range(1, quads):
            total = total + got_ref[i, u].astype(F32)
        total = total.astype(BF16)
        for block in range(columns // 128):
            start = (block * members + u) * 128
            out_ref[:, start : start + 128] = total[:, block * 128 : (block + 1) * 128]


def on_device(queries, keys, values, coef_table, level_index, out_weight):
    rows, key_size = queries.shape
    value_size = values.shape[1]
    x = lax.axis_index("x")
    u = lax.axis_index(QUAD)
    nx, ny, nu = lax.axis_size("x"), lax.axis_size("y"), 4

    state = lax.dot_general(keys, values, (((0,), (0,)), ((), ())), preferred_element_type=F32)
    half, piece = key_size // 2, key_size // nx
    odd, high = x % 2, x // 2
    given = lax.dynamic_slice_in_dim(state, (1 - odd) * half, half).astype(BF16)
    kept = lax.dynamic_slice_in_dim(state, odd * half, half)
    one = crossed(given, "x", 1)

    got = []
    for k in range(nu):
        pairs = [(i * nu + j, (j ^ k) * nu + i) for i in range(nx) for j in range(nu)]
        got.append(lax.ppermute(out_weight, ("x",) + QUAD, pairs))

    *got, one = lax.optimization_barrier((*got, one))
    weight = jnp.stack(got)
    gathered = lax.all_gather(weight, "y", axis=0)

    halves = kept + one.astype(F32)
    given = lax.dynamic_slice_in_dim(halves, (1 - high) * piece, piece).astype(BF16)
    quarter = lax.dynamic_slice_in_dim(halves, high * piece, piece)
    part = crossed(given, "x", 2)
    quarter = quarter + part.astype(F32)
    beside = crossed(quarter.astype(BF16), "y", 1)

    late, part = lax.optimization_barrier((kept.astype(BF16), part))
    rest = crossed(late, "x", 1)
    near = jnp.where(odd == 1, jnp.concatenate([rest, one]), jnp.concatenate([one, rest]))
    pair = crossed((state + near.astype(F32)).astype(BF16), "x", 2)

    local, lam = pl.pallas_call(
        local_kernel,
        out_shape=(
            jax.ShapeDtypeStruct((rows, value_size), F32),
            jax.ShapeDtypeStruct(level_index.shape, F32),
        ),
        in_specs=[SMEM] + [VMEM] * 4,
        out_specs=(VMEM, VMEM),
        compiler_params=PARAMS,
    )(coef_table, level_index, queries, keys, values)

    beside, local = lax.optimization_barrier((beside, local))
    both = (quarter + beside.astype(F32)).astype(BF16)
    third, fourth, fifth = crossed(both, "y", 2), crossed(both, "y", 4), crossed(both, "y", 6)
    far = [beside, third, (fourth.astype(F32) + fifth.astype(F32)).astype(BF16)]
    far = lax.all_gather(jnp.stack(far), "x", axis=0)

    levels = level_index.shape[1]
    block = lax.axis_index(CTX).astype(jnp.int32).reshape(1)
    o = pl.pallas_call(
        functools.partial(inter_kernel, levels - 2 - far.shape[1]),
        out_shape=jax.ShapeDtypeStruct((rows, value_size), BF16),
        in_specs=[SMEM] + [VMEM] * 6,
        out_specs=VMEM,
        compiler_params=PARAMS,
    )(block, local, lam, queries, near, pair, far)

    o_z = flipped(o, "zl")
    o_c = flipped(o, "core")
    o_zc = flipped(o_z, "core")
    flip = jnp.bitwise_xor(x, u).astype(jnp.int32).reshape(1)
    width = out_weight.shape[1]
    part = pl.pallas_call(
        project_kernel,
        out_shape=jax.ShapeDtypeStruct((rows, ny * width), BF16),
        in_specs=[SMEM] + [VMEM] * 4 + [pl.BlockSpec(memory_space=pl.ANY)],
        out_specs=VMEM,
        scratch_shapes=[
            pltpu.VMEM((ny, nu, value_size, width), BF16),
            pltpu.SemaphoreType.DMA((ny // 2,)),
        ],
        compiler_params=PARAMS,
    )(flip, o, o_c, o_z, o_zc, gathered)

    n = lax.axis_size(TP)
    back = lax.all_to_all(part, TP, 0, 0, tiled=True)
    return pl.pallas_call(
        sum_kernel,
        out_shape=jax.ShapeDtypeStruct((rows // n, nu * ny * width), BF16),
        in_specs=[VMEM],
        out_specs=VMEM,
        compiler_params=PARAMS,
    )(back.reshape(n // nu, nu, rows // n, ny * width))


def solution(mesh):
    split = Mesh(mesh.devices.reshape(8, 4, 4, 2, 2), CTX + TP)
    in_specs = (P(CTX, TP), P(CTX, TP), P(CTX, TP), P(None, TP), P(CTX, None), P(TP, CTX))
    out_specs = P(CTX + TP, None)
    return jax.shard_map(on_device, mesh=split, in_specs=in_specs, out_specs=out_specs, check_vma=False)
```

```python
import functools

import jax
import jax.numpy as jnp
from jax import lax
from jax.experimental import pallas as pl
from jax.experimental.pallas import tpu as pltpu
from jax.sharding import Mesh, PartitionSpec as P

F32, BF16 = jnp.float32, jnp.bfloat16
QUAD = ("zl", "core")
TP = ("zh", "zl", "core")
CTX = ("y", "x")
VMEM = pl.BlockSpec(memory_space=pltpu.VMEM)
SMEM = pl.BlockSpec(memory_space=pltpu.SMEM)
PARAMS = pltpu.CompilerParams(vmem_limit_bytes=48 * 1024 * 1024)


def shifted(value, axis, by):
    n = lax.axis_size(axis)
    return lax.ppermute(value, axis, [(i, (i + by) % n) for i in range(n)])


def crossed(value, axis, by):
    return lax.ppermute(value, axis, [(i, i ^ by) for i in range(lax.axis_size(axis))])


def onward(value, axis, by, bit):
    pairs = [(i, i ^ by) for i in range(lax.axis_size(axis)) if not i & bit]
    return lax.ppermute(value, axis, pairs)


def flipped(value, axis):
    return lax.ppermute(value, axis, [(0, 1), (1, 0)])


def local_kernel(coef_ref, index_ref, q_ref, k_ref, v_ref, local_ref, lam_ref):
    index = index_ref[...]
    lam = jnp.zeros(index.shape, F32)
    for row in range(coef_ref.shape[0]):
        lam = jnp.where(index == row, coef_ref[row, 0], lam)
    level_of = lax.broadcasted_iota(jnp.int32, index.shape, 1).astype(F32)
    lam = lam * jnp.exp2(-0.5 * level_of)
    lam_ref[...] = lam
    inverse_scale = 1.0 / q_ref.shape[1] ** 0.5
    tile = 128
    t = lax.broadcasted_iota(jnp.int32, (tile, tile), 0)
    s = lax.broadcasted_iota(jnp.int32, (tile, tile), 1)
    crossed = jnp.bitwise_xor(t, s)
    causal = t >= s
    for i in range(q_ref.shape[0] // tile):
        rows = slice(i * tile, (i + 1) * tile)
        lam_rows = lam[rows]
        scores = lax.dot_general(
            q_ref[rows, :], k_ref[: (i + 1) * tile, :], (((1,), (1,)), ((), ())), preferred_element_type=F32
        )
        scores = scores * inverse_scale
        pieces = []
        for j in range(i):
            level = 7 + (i ^ j).bit_length()
            pieces.append(scores[:, j * tile : (j + 1) * tile] * lam_rows[:, level : level + 1])
        weight = jnp.broadcast_to(lam_rows[:, 0:1], (tile, tile))
        for bit in range(7):
            weight = jnp.where(crossed >= 2**bit, lam_rows[:, bit + 1 : bit + 2], weight)
        weight = jnp.where(causal, weight, 0.0)
        pieces.append(scores[:, i * tile :] * weight)
        attn = jnp.concatenate([piece.astype(BF16) for piece in pieces], axis=1)
        local_ref[rows, :] = jnp.dot(attn, v_ref[: (i + 1) * tile, :], preferred_element_type=F32)


def inter_kernel(base, bits_ref, local_ref, lam_ref, q_ref, near_ref, pair_ref, far_ref, o_ref):
    q = q_ref[...]
    inverse_scale = 1.0 / q.shape[1] ** 0.5
    total = local_ref[...]
    count = 2 + far_ref.shape[1]
    for bit in range(count):
        if bit == 0:
            node = near_ref[...]
        elif bit == 1:
            node = pair_ref[...]
        else:
            node = jnp.concatenate([far_ref[i, bit - 2] for i in (0, 2, 1, 3)], axis=0)
        setbit = (bits_ref[0] >> bit & 1).astype(F32)
        factor = lam_ref[:, base + bit : base + bit + 1] * inverse_scale * setbit
        total = total + jnp.dot(q, node, preferred_element_type=F32) * factor
    o_ref[...] = total.astype(BF16)


def project_kernel(flip_ref, o0_ref, o1_ref, o2_ref, o3_ref, w_ref, part_ref):
    total = None
    for j, o_ref in enumerate((o0_ref, o1_ref, o2_ref, o3_ref)):
        k = jnp.bitwise_xor(flip_ref[0], j)
        w = jnp.concatenate([w_ref[0, k], w_ref[1, k]], axis=1)
        term = jnp.dot(o_ref[...], w, preferred_element_type=F32)
        total = term if total is None else total + term
    part_ref[...] = total.astype(BF16)


def sum_kernel(got_ref, out_ref):
    quads, members, _, columns = got_ref.shape
    for u in range(members):
        total = got_ref[0, u].astype(F32)
        for i in range(1, quads):
            total = total + got_ref[i, u].astype(F32)
        total = total.astype(BF16)
        for block in range(columns // 128):
            start = (block * members + u) * 128
            out_ref[:, start : start + 128] = total[:, block * 128 : (block + 1) * 128]


def on_device(queries, keys, values, coef_table, level_index, out_weight):
    rows, key_size = queries.shape
    value_size = values.shape[1]
    x = lax.axis_index("x")
    u = lax.axis_index(QUAD)
    nx, ny, nu = lax.axis_size("x"), lax.axis_size("y"), 4

    state = lax.dot_general(keys, values, (((0,), (0,)), ((), ())), preferred_element_type=F32)
    half, piece = key_size // 2, key_size // nx
    odd, high = x % 2, x // 2
    given = lax.dynamic_slice_in_dim(state, (1 - odd) * half, half).astype(BF16)
    kept = lax.dynamic_slice_in_dim(state, odd * half, half)
    one = crossed(given, "x", 1)

    got = []
    for k in range(nu):
        pairs = [(i * nu + j, (j ^ k) * nu + i) for i in range(nx) for j in range(nu)]
        got.append(lax.ppermute(out_weight, ("x",) + QUAD, pairs))

    *got, one = lax.optimization_barrier((*got, one))
    weight = jnp.stack(got)
    gathered = lax.all_gather(weight, "y", axis=0)

    halves = kept + one.astype(F32)
    given = lax.dynamic_slice_in_dim(halves, (1 - high) * piece, piece).astype(BF16)
    quarter = lax.dynamic_slice_in_dim(halves, high * piece, piece)
    part = crossed(given, "x", 2)
    quarter = quarter + part.astype(F32)
    beside = crossed(quarter.astype(BF16), "y", 1)

    late, part = lax.optimization_barrier((kept.astype(BF16), part))
    rest = crossed(late, "x", 1)
    near = jnp.where(odd == 1, jnp.concatenate([rest, one]), jnp.concatenate([one, rest]))
    pair = onward((state + near.astype(F32)).astype(BF16), "x", 2, 2)

    local, lam = pl.pallas_call(
        local_kernel,
        out_shape=(
            jax.ShapeDtypeStruct((rows, value_size), F32),
            jax.ShapeDtypeStruct(level_index.shape, F32),
        ),
        in_specs=[SMEM] + [VMEM] * 4,
        out_specs=(VMEM, VMEM),
        compiler_params=PARAMS,
    )(coef_table, level_index, queries, keys, values)

    beside, local = lax.optimization_barrier((beside, local))
    both = (quarter + beside.astype(F32)).astype(BF16)
    third, fourth, fifth = onward(both, "y", 2, 2), onward(both, "y", 4, 4), onward(both, "y", 6, 4)
    far = [beside, third, (fourth.astype(F32) + fifth.astype(F32)).astype(BF16)]
    far = lax.all_gather(jnp.stack(far), "x", axis=0)

    levels = level_index.shape[1]
    block = lax.axis_index(CTX).astype(jnp.int32).reshape(1)
    o = pl.pallas_call(
        functools.partial(inter_kernel, levels - 2 - far.shape[1]),
        out_shape=jax.ShapeDtypeStruct((rows, value_size), BF16),
        in_specs=[SMEM] + [VMEM] * 6,
        out_specs=VMEM,
        compiler_params=PARAMS,
    )(block, local, lam, queries, near, pair, far)

    o_z = flipped(o, "zl")
    o_c = flipped(o, "core")
    o_zc = flipped(o_z, "core")
    flip = jnp.bitwise_xor(x, u).astype(jnp.int32).reshape(1)
    width = out_weight.shape[1]
    whole = pl.BlockSpec((rows, value_size), lambda i: (0, 0))
    part = pl.pallas_call(
        project_kernel,
        grid=(ny // 2,),
        out_shape=jax.ShapeDtypeStruct((rows, ny * width), BF16),
        in_specs=[SMEM]
        + [whole] * 4
        + [pl.BlockSpec((2, nu, value_size, width), lambda i: (i, 0, 0, 0))],
        out_specs=pl.BlockSpec((rows, 2 * width), lambda i: (0, i)),
        compiler_params=PARAMS,
    )(flip, o, o_c, o_z, o_zc, gathered)

    n = lax.axis_size(TP)
    back = lax.all_to_all(part, TP, 0, 0, tiled=True)
    return pl.pallas_call(
        sum_kernel,
        out_shape=jax.ShapeDtypeStruct((rows // n, nu * ny * width), BF16),
        in_specs=[VMEM],
        out_specs=VMEM,
        compiler_params=PARAMS,
    )(back.reshape(n // nu, nu, rows // n, ny * width))


def solution(mesh):
    split = Mesh(mesh.devices.reshape(8, 4, 4, 2, 2), CTX + TP)
    in_specs = (P(CTX, TP), P(CTX, TP), P(CTX, TP), P(None, TP), P(CTX, None), P(TP, CTX))
    out_specs = P(CTX + TP, None)
    return jax.shard_map(on_device, mesh=split, in_specs=in_specs, out_specs=out_specs, check_vma=False)
```

```python
import functools

import jax
import jax.numpy as jnp
from jax import lax
from jax.experimental import pallas as pl
from jax.experimental.pallas import tpu as pltpu
from jax.sharding import Mesh, PartitionSpec as P

F32, BF16 = jnp.float32, jnp.bfloat16
QUAD = ("zl", "core")
TP = ("zh", "zl", "core")
CTX = ("y", "x")
VMEM = pl.BlockSpec(memory_space=pltpu.VMEM)
SMEM = pl.BlockSpec(memory_space=pltpu.SMEM)
PARAMS = pltpu.CompilerParams(vmem_limit_bytes=48 * 1024 * 1024)


def shifted(value, axis, by):
    n = lax.axis_size(axis)
    return lax.ppermute(value, axis, [(i, (i + by) % n) for i in range(n)])


def crossed(value, axis, by):
    return lax.ppermute(value, axis, [(i, i ^ by) for i in range(lax.axis_size(axis))])


def onward(value, axis, by, bit):
    pairs = [(i, i ^ by) for i in range(lax.axis_size(axis)) if not i & bit]
    return lax.ppermute(value, axis, pairs)


def flipped(value, axis):
    return lax.ppermute(value, axis, [(0, 1), (1, 0)])


def local_kernel(coef_ref, index_ref, q_ref, k_ref, v_ref, local_ref, lam_ref):
    index = index_ref[...]
    lam = jnp.zeros(index.shape, F32)
    for row in range(coef_ref.shape[0]):
        lam = jnp.where(index == row, coef_ref[row, 0], lam)
    level_of = lax.broadcasted_iota(jnp.int32, index.shape, 1).astype(F32)
    lam = lam * jnp.exp2(-0.5 * level_of)
    lam_ref[...] = lam
    inverse_scale = 1.0 / q_ref.shape[1] ** 0.5
    tile = 128
    t = lax.broadcasted_iota(jnp.int32, (tile, tile), 0)
    s = lax.broadcasted_iota(jnp.int32, (tile, tile), 1)
    crossed = jnp.bitwise_xor(t, s)
    causal = t >= s
    for i in range(q_ref.shape[0] // tile):
        rows = slice(i * tile, (i + 1) * tile)
        lam_rows = lam[rows]
        scores = lax.dot_general(
            q_ref[rows, :], k_ref[: (i + 1) * tile, :], (((1,), (1,)), ((), ())), preferred_element_type=F32
        )
        scores = scores * inverse_scale
        pieces = []
        for j in range(i):
            level = 7 + (i ^ j).bit_length()
            pieces.append(scores[:, j * tile : (j + 1) * tile] * lam_rows[:, level : level + 1])
        weight = jnp.broadcast_to(lam_rows[:, 0:1], (tile, tile))
        for bit in range(7):
            weight = jnp.where(crossed >= 2**bit, lam_rows[:, bit + 1 : bit + 2], weight)
        weight = jnp.where(causal, weight, 0.0)
        pieces.append(scores[:, i * tile :] * weight)
        attn = jnp.concatenate([piece.astype(BF16) for piece in pieces], axis=1)
        local_ref[rows, :] = jnp.dot(attn, v_ref[: (i + 1) * tile, :], preferred_element_type=F32)


def inter_kernel(base, bits_ref, local_ref, lam_ref, q_ref, near_ref, pair_ref, far_ref, o_ref):
    q = q_ref[...]
    inverse_scale = 1.0 / q.shape[1] ** 0.5
    total = local_ref[...]
    count = 2 + far_ref.shape[1]
    for bit in range(count):
        if bit == 0:
            node = near_ref[...]
        elif bit == 1:
            node = pair_ref[...]
        else:
            node = jnp.concatenate([far_ref[i, bit - 2] for i in (0, 2, 1, 3)], axis=0)
        setbit = (bits_ref[0] >> bit & 1).astype(F32)
        factor = lam_ref[:, base + bit : base + bit + 1] * inverse_scale * setbit
        total = total + jnp.dot(q, node, preferred_element_type=F32) * factor
    o_ref[...] = total.astype(BF16)


def project_kernel(flip_ref, o0_ref, o1_ref, o2_ref, o3_ref, w_ref, part_ref):
    total = None
    for j, o_ref in enumerate((o0_ref, o1_ref, o2_ref, o3_ref)):
        k = jnp.bitwise_xor(flip_ref[0], j)
        w = jnp.concatenate([w_ref[0, k], w_ref[1, k]], axis=1)
        term = jnp.dot(o_ref[...], w, preferred_element_type=F32)
        total = term if total is None else total + term
    part_ref[...] = total.astype(BF16)


def sum_kernel(got_ref, out_ref):
    quads, members, _, columns = got_ref.shape
    for u in range(members):
        total = got_ref[0, u].astype(F32)
        for i in range(1, quads):
            total = total + got_ref[i, u].astype(F32)
        total = total.astype(BF16)
        for block in range(columns // 128):
            start = (block * members + u) * 128
            out_ref[:, start : start + 128] = total[:, block * 128 : (block + 1) * 128]


def on_device(queries, keys, values, coef_table, level_index, out_weight):
    rows, key_size = queries.shape
    value_size = values.shape[1]
    x = lax.axis_index("x")
    u = lax.axis_index(QUAD)
    nx, ny, nu = lax.axis_size("x"), lax.axis_size("y"), 4

    state = lax.dot_general(keys, values, (((0,), (0,)), ((), ())), preferred_element_type=F32)
    half, piece = key_size // 2, key_size // nx
    odd, high = x % 2, x // 2
    given = lax.dynamic_slice_in_dim(state, (1 - odd) * half, half).astype(BF16)
    kept = lax.dynamic_slice_in_dim(state, odd * half, half)
    one = crossed(given, "x", 1)

    got = []
    for k in range(nu):
        pairs = [(i * nu + j, (j ^ k) * nu + i) for i in range(nx) for j in range(nu)]
        got.append(lax.ppermute(out_weight, ("x",) + QUAD, pairs))

    *got, one = lax.optimization_barrier((*got, one))
    weight = jnp.stack(got)
    gathered = lax.all_gather(weight, "y", axis=0)

    halves = kept + one.astype(F32)
    given = lax.dynamic_slice_in_dim(halves, (1 - high) * piece, piece).astype(BF16)
    quarter = lax.dynamic_slice_in_dim(halves, high * piece, piece)
    part = crossed(given, "x", 2)
    quarter = quarter + part.astype(F32)
    beside = crossed(quarter.astype(BF16), "y", 1)

    late, part = lax.optimization_barrier((kept.astype(BF16), part))
    rest = lax.ppermute(late, "x", [(0, 1), (1, 0), (2, 3)])
    near = jnp.where(odd == 1, jnp.concatenate([rest, one]), jnp.concatenate([one, rest]))
    pair = onward((state + near.astype(F32)).astype(BF16), "x", 2, 2)

    local, lam = pl.pallas_call(
        local_kernel,
        out_shape=(
            jax.ShapeDtypeStruct((rows, value_size), F32),
            jax.ShapeDtypeStruct(level_index.shape, F32),
        ),
        in_specs=[SMEM] + [VMEM] * 4,
        out_specs=(VMEM, VMEM),
        compiler_params=PARAMS,
    )(coef_table, level_index, queries, keys, values)

    beside, local = lax.optimization_barrier((beside, local))
    both = (quarter + beside.astype(F32)).astype(BF16)
    third, fourth, fifth = onward(both, "y", 2, 2), onward(both, "y", 4, 4), onward(both, "y", 6, 4)
    far = [beside, third, (fourth.astype(F32) + fifth.astype(F32)).astype(BF16)]
    far = lax.all_gather(jnp.stack(far), "x", axis=0)

    levels = level_index.shape[1]
    block = lax.axis_index(CTX).astype(jnp.int32).reshape(1)
    o = pl.pallas_call(
        functools.partial(inter_kernel, levels - 2 - far.shape[1]),
        out_shape=jax.ShapeDtypeStruct((rows, value_size), BF16),
        in_specs=[SMEM] + [VMEM] * 6,
        out_specs=VMEM,
        compiler_params=PARAMS,
    )(block, local, lam, queries, near, pair, far)

    o_z = flipped(o, "zl")
    o_c = flipped(o, "core")
    o_zc = flipped(o_z, "core")
    flip = jnp.bitwise_xor(x, u).astype(jnp.int32).reshape(1)
    width = out_weight.shape[1]
    part = pl.pallas_call(
        project_kernel,
        grid=(ny // 2,),
        out_shape=jax.ShapeDtypeStruct((rows, ny * width), BF16),
        in_specs=[SMEM]
        + [VMEM] * 4
        + [pl.BlockSpec((2, nu, value_size, width), lambda i: (i, 0, 0, 0))],
        out_specs=pl.BlockSpec((rows, 2 * width), lambda i: (0, i)),
        compiler_params=PARAMS,
    )(flip, o, o_c, o_z, o_zc, gathered)

    n = lax.axis_size(TP)
    back = lax.all_to_all(part, TP, 0, 0, tiled=True)
    return pl.pallas_call(
        sum_kernel,
        out_shape=jax.ShapeDtypeStruct((rows // n, nu * ny * width), BF16),
        in_specs=[VMEM],
        out_specs=VMEM,
        compiler_params=PARAMS,
    )(back.reshape(n // nu, nu, rows // n, ny * width))


def solution(mesh):
    split = Mesh(mesh.devices.reshape(8, 4, 4, 2, 2), CTX + TP)
    in_specs = (P(CTX, TP), P(CTX, TP), P(CTX, TP), P(None, TP), P(CTX, None), P(TP, CTX))
    out_specs = P(CTX + TP, None)
    return jax.shard_map(on_device, mesh=split, in_specs=in_specs, out_specs=out_specs, check_vma=False)
```
